256 devices in a mesh: grp: 16 (over x, y), tp: 16 (over z, core).
Axes of the slice: x: 4, y: 4, z: 8, core: 2. Of those that a mesh axis runs over, the one named last changes fastest.
Arguments:
- tokens: bfloat16 [12288, 3584], P(('grp', 'tp')), parts along dimension 0, may hold values from -6 to 6
- counts: int32 [256], P(('grp', 'tp')), parts along dimension 0, may hold values from 16 to 48, as said below
- norm_gain: float32 [3584], replicated, may hold values from 0.1 to 1.9
- gate_weight: bfloat16 [3584, 9216], P(None, 'tp'), may hold values from -0.09375 to 0.09375
- up_weight: bfloat16 [3584, 9216], P(None, 'tp'), may hold values from -0.09375 to 0.09375
- down_weight: bfloat16 [9216, 3584], P('tp'), may hold values from -0.0625 to 0.0625
Outputs:
- mixed: bfloat16 [12288, 3584], P(('grp', 'tp')), parts along dimension 0
The draws below stay inside these ranges and needn't reach their ends.
There are 16 independent parts, one for each index of `grp`. The reference program is written for one: setup_inputs(seed, part) draws one part's arguments, and reference() takes and returns one part's arrays. A program takes and returns all parts, laid end to end along the dimension named above; an argument that names none is the same for every part. Nothing has to cross between parts.
Inputs may be any that keep to these rules, and one draw needn't show every extreme that they name: `counts`: each device holds from 16 to 48 live requests in its first slots; in every group some device holds exactly 48 and another exactly 16.
All inputs are finite; a program needn't handle non-finite values.
Results may differ from the reference program's by a relative error of at most 0.023.
Values may be sent and summed in bfloat16 or wider, within the bound.
No kernel may reach another device: no remote copies, remote signals or barrier semaphores. Data moves between devices by JAX's collectives and lax.ppermute only.
A program may use at most 64 MiB of HBM per device.

```python
import jax
import jax.numpy as jnp
from jax import lax

D = 3584
FF = 9216
SLOTS = 48
MINREQ = 16
ROWS = 768
FF_DEV = 576
N_TP = 16


def draw_counts(key, part):
    key = jax.random.fold_in(key, 11)
    key_base, key_top, key_low = jax.random.split(key, 3)
    base_counts = jax.random.randint(key_base, (N_TP,), MINREQ, SLOTS + 1)
    top_device = jax.random.randint(key_top, (), 0, N_TP)
    low_device = (top_device + 1 + jax.random.randint(key_low, (), 0, N_TP - 1)) % N_TP
    device_ids = jnp.arange(N_TP, dtype=jnp.int32)
    base_counts = jnp.where(device_ids == top_device, SLOTS, base_counts)
    base_counts = jnp.where(device_ids == low_device, MINREQ, base_counts)
    return base_counts.astype(jnp.int32)


def block_scale(stream_key, shape, cuts, least, high):
    def one(position, parts):
        heights = jax.random.uniform(jax.random.fold_in(jax.random.fold_in(stream_key, 6), position), (parts,), jnp.float32, least / len(cuts), high / len(cuts))
        return jnp.repeat(jnp.exp(heights), shape[position] // parts).reshape((-1,) + (1,) * (len(shape) - position - 1))

    factor_of = one(*cuts[0])
    for cut in cuts[1:]:
        factor_of = factor_of * one(*cut)
    return factor_of


def noise(rng, dims, width, reach, cuts=(), kind=jnp.bfloat16):
    loudness = block_scale(rng, dims, cuts, -0.22, 0.18) if cuts else 1.0
    entries = jax.random.normal(rng, dims, jnp.float32) * width * loudness
    return jnp.minimum(jnp.maximum(entries, -reach), reach).astype(kind)


def setup_inputs(seed: int = 0, part: int = 0) -> dict:
    key_list = jax.random.split(jax.random.key(seed), 7)
    part_splits = jax.random.split(jax.random.fold_in(key_list[6], part), 7)
    tokens = noise(part_splits[0], (ROWS, D), 1.0, 6.0, ((0, 16),))
    counts = draw_counts(jax.random.fold_in(jax.random.fold_in(key_list[6], part), 71), part)
    norm_gain = jnp.clip(1.0 + 0.18 * jax.random.normal(key_list[2], (D,), jnp.float32), 0.1, 1.9)
    gate_weight = noise(key_list[3], (D, FF), D ** -0.5, 0.09375, ((1, 16),))
    up_weight = noise(key_list[4], (D, FF), D ** -0.5, 0.09375, ((1, 16),))
    down_weight = noise(key_list[5], (FF, D), FF ** -0.5, 0.0625, ((0, 16),))
    return dict(tokens=tokens, counts=counts, norm_gain=norm_gain, gate_weight=gate_weight, up_weight=up_weight, down_weight=down_weight)


def reference(tokens, counts, norm_gain, gate_weight, up_weight, down_weight):
    widened = tokens.astype(jnp.float32)
    scale_row = lax.rsqrt(lax.optimization_barrier(jnp.mean(widened * widened, axis=-1, keepdims=True)) + 1e-06)
    normed = (widened * scale_row * norm_gain.astype(jnp.float32)).astype(jnp.bfloat16)
    gate = jnp.dot(normed, gate_weight, preferred_element_type=jnp.float32)
    up_part = jnp.dot(normed, up_weight, preferred_element_type=jnp.float32)
    hidden = (jax.nn.silu(gate) * up_part).astype(jnp.bfloat16)
    row_total = tokens.shape[0]
    summed = jnp.zeros((row_total, tokens.shape[1]), jnp.float32)
    for group in range(N_TP):
        block_cols = hidden[:, group * FF_DEV:(group + 1) * FF_DEV]
        block_rows = down_weight[group * FF_DEV:(group + 1) * FF_DEV]
        partial_value = jnp.dot(block_cols, block_rows, preferred_element_type=jnp.float32).astype(jnp.bfloat16)
        partial_value = lax.optimization_barrier(partial_value)
        summed = summed + partial_value.astype(jnp.float32)
    row_index = jnp.arange(row_total, dtype=jnp.int32)
    slot_index = row_index % SLOTS
    owner_index = row_index // SLOTS
    alive_mask = slot_index < counts[owner_index]
    return jnp.where(alive_mask[:, None], summed, 0.0).astype(jnp.bfloat16)
```

```python
import jax
import jax.numpy as jnp
from jax import lax
from jax.experimental import pallas as pl
from jax.experimental.pallas import tpu as pltpu
from jax.sharding import PartitionSpec as P

CHUNKS = 3
HOP_BYTES = 9_000_000
IN_VMEM = pl.BlockSpec(memory_space=pltpu.VMEM)


def local(kernel, shape, operands, specs=None, bytes_accessed=HOP_BYTES):
    return pl.pallas_call(
        kernel,
        out_shape=jax.ShapeDtypeStruct(shape, jnp.bfloat16),
        in_specs=specs or [IN_VMEM] * len(operands),
        out_specs=IN_VMEM,
        compiler_params=pltpu.CompilerParams(vmem_limit_bytes=3 << 20),
        cost_estimate=pl.CostEstimate(flops=0, bytes_accessed=bytes_accessed, transcendentals=0),
    )(*operands)


def normalize(tokens, gain):
    slots, width = tokens.shape

    def kernel(tokens_ref, gain_ref, normed_ref):
        for at in range(0, slots, 16):
            rows = pl.ds(at, 16)
            widened = tokens_ref[rows, :].astype(jnp.float32)
            scale_row = lax.rsqrt(jnp.sum(widened * widened, axis=-1, keepdims=True) / width + 1e-06)
            normed_ref[rows, :] = (widened * scale_row * gain_ref[...]).astype(normed_ref.dtype)

    return local(kernel, tokens.shape, (tokens, gain.reshape(1, width)))


def join(size, *terms):
    spans = [(at, rows) for _, at, rows in terms]

    def kernel(*refs):
        cut = min(rows for _, rows in spans)
        for low, high in ((0, cut), (cut, size)):
            if low < high:
                total = None
                for ref, (at, rows) in zip(refs, spans):
                    if rows >= high:
                        value = ref[pl.ds(at + low, high - low), :].astype(jnp.float32)
                        total = value if total is None else total + value
                refs[-1][pl.ds(low, high - low), :] = total.astype(refs[-1].dtype)

    return local(kernel, (size, terms[0][0].shape[1]), [array for array, _, _ in terms])


def body(tokens, counts, norm_gain, gate_weight, up_weight, down_weight):
    slots, width = tokens.shape
    members = lax.axis_size("tp")
    chips = members // 2
    part = slots // CHUNKS
    both = 2 * part

    swap_pairs = [(i, i ^ 1) for i in range(members)]
    ring_pairs = [(2 * z, 2 * ((z + 1) % chips)) for z in range(chips)]
    ring_pairs += [(2 * z + 1, 2 * ((z - 1) % chips) + 1) for z in range(chips)]

    def swap(value):
        return lax.ppermute(value, "tp", swap_pairs)

    def ring(value):
        return lax.ppermute(value, "tp", ring_pairs)

    f32 = jnp.float32
    bf16 = jnp.bfloat16
    token = counts

    def order(*values):
        nonlocal token
        token, *values = lax.optimization_barrier((token, *values))
        return values if len(values) > 1 else values[0]

    def concat(*values):
        return order(jnp.concatenate(order(*values), 0))

    batch = {}

    def gate_of(name):
        rows, weight = order(batch[name], gate_weight)
        batch[name] = rows, order(jnp.dot(rows, weight, preferred_element_type=f32))

    def hidden_of(name):
        rows, gate, weight = order(*batch[name], up_weight)
        up_part = jnp.dot(rows, weight, preferred_element_type=f32)
        batch[name] = order((jax.nn.silu(gate) * up_part).astype(bf16))

    def partial_of(name):
        hidden, weight = order(batch[name], down_weight)
        batch[name] = order(jnp.dot(hidden, weight, preferred_element_type=f32).astype(bf16))

    chunks = range(CHUNKS)
    normed = order(normalize(*order(tokens, norm_gain)))
    swapped = order(swap(normed))
    own, flight = [], []
    for i in chunks:
        rows = slice(i * part, (i + 1) * part)
        own.append(concat(normed[rows], swapped[rows]))
        flight.append(ring(own[i]))

    mine = {}
    other = {}

    def arrive(hop, i):
        block = order(flight[i])
        mine[hop, i] = block
        if hop < 3:
            flight[i] = ring(block)
        elif hop == 3:
            flight[i] = ring(block[:part])

    arrive(1, 0)
    arrive(1, 1)
    arrive(1, 2)
    other[1] = swap(concat(*[mine[1, i] for i in chunks]))
    arrive(2, 0)
    other[1] = order(other[1])
    batch["a"] = concat(*own, *[mine[1, i] for i in chunks], other[1][:2 * both])
    gate_of("a")
    arrive(2, 1)
    hidden_of("a")
    arrive(2, 2)
    other[2] = swap(concat(*[mine[2, i] for i in chunks]))
    partial_of("a")
    arrive(3, 0)
    moved_1 = swap(batch["a"][3 * both:6 * both])
    other[2] = order(other[2])
    batch["b"] = concat(other[1][2 * both:], other[2], *[mine[2, i] for i in chunks], mine[3, 0])
    gate_of("b")
    arrive(3, 1)
    moved_1 = order(moved_1)
    hidden_of("b")
    arrive(3, 2)
    other[3] = swap(concat(*[mine[3, i] for i in chunks]))
    partial_of("b")
    moved_2 = swap(batch["b"][4 * both:])
    other[3] = order(other[3])
    arrive(4, 0)
    moved_2 = order(moved_2)
    arrive(4, 1)
    arrive(4, 2)
    fourth = concat(*[mine[4, i] for i in chunks])
    other[4] = order(swap(fourth))
    batch["c"] = concat(other[3], mine[3, 1], mine[3, 2], fourth, other[4])
    gate_of("c")
    hidden_of("c")
    partial_of("c")
    moved_4 = swap(batch["c"][5 * both:5 * both + 3 * part])
    moved_3 = swap(batch["c"][3 * both:5 * both])
    moved_4 = order(moved_4)

    def depart(hop, i):
        size = part if hop == 4 else both
        terms = []
        if hop == 4:
            terms = [(batch["c"], 5 * both + 3 * part + i * part, part), (moved_4, i * part, part)]
        elif hop == 3:
            there = (moved_2, 3 * both, both) if i == 0 else (moved_3, (i - 1) * both, both)
            terms = [(batch["c"], i * both, both), there, (flight[i], 0, part)]
        elif hop == 2:
            terms = [(batch["b"], (1 + i) * both, both), (moved_2, i * both, both), (flight[i], 0, both)]
        elif hop == 1:
            here = (batch["b"], 0, both) if i == 2 else (batch["a"], (6 + i) * both, both)
            terms = [here, (moved_1, i * both, both), (flight[i], 0, both)]
        arrays = order(*[array for array, _, _ in terms])
        terms = [(array, at, rows) for array, (_, at, rows) in zip(arrays, terms)]
        flight[i] = ring(order(join(size, *terms)))

    for i in chunks:
        depart(4, i)
    moved_3 = order(moved_3)
    for hop in (3, 2, 1):
        for i in chunks:
            depart(hop, i)
    given = []
    for i in chunks:
        carry, mixed = order(flight[i], batch["a"])
        flight[i] = carry
        given.append(swap(order(join(part, (mixed, i * both + part, part), (carry, 0, part)))))
    done = []
    for i in chunks:
        carry, mixed, gift = order(flight[i], batch["a"], given[i])
        done.append(carry[part:].astype(f32) + mixed[i * both:i * both + part].astype(f32) + gift.astype(f32))
    alive = jnp.arange(slots, dtype=jnp.int32) < token[0]
    return jnp.where(alive[:, None], jnp.concatenate(done, 0), 0.0).astype(bf16)


def solution(mesh):
    in_specs = (
        P(("grp", "tp"), None),
        P(("grp", "tp")),
        P(),
        P(None, "tp"),
        P(None, "tp"),
        P("tp", None),
    )
    out_specs = P(("grp", "tp"), None)
    return jax.shard_map(body, mesh=mesh, in_specs=in_specs, out_specs=out_specs, check_vma=False)
```

```python
import jax
import jax.numpy as jnp
from jax import lax
from jax.experimental import pallas as pl
from jax.experimental.pallas import tpu as pltpu
from jax.sharding import PartitionSpec as P

CHUNKS = 3
HOP_BYTES = 9_000_000
IN_VMEM = pl.BlockSpec(memory_space=pltpu.VMEM)


def local(kernel, shape, operands, specs=None, bytes_accessed=HOP_BYTES):
    return pl.pallas_call(
        kernel,
        out_shape=jax.ShapeDtypeStruct(shape, jnp.bfloat16),
        in_specs=specs or [IN_VMEM] * len(operands),
        out_specs=IN_VMEM,
        compiler_params=pltpu.CompilerParams(vmem_limit_bytes=3 << 20),
        cost_estimate=pl.CostEstimate(flops=0, bytes_accessed=bytes_accessed, transcendentals=0),
    )(*operands)


def normalize(tokens, gain):
    slots, width = tokens.shape

    def kernel(tokens_ref, gain_ref, normed_ref):
        for at in range(0, slots, 16):
            rows = pl.ds(at, 16)
            widened = tokens_ref[rows, :].astype(jnp.float32)
            scale_row = lax.rsqrt(jnp.sum(widened * widened, axis=-1, keepdims=True) / width + 1e-06)
            normed_ref[rows, :] = (widened * scale_row * gain_ref[...].reshape(1, width)).astype(normed_ref.dtype)

    return local(kernel, tokens.shape, (tokens, gain))


def pack(*blocks):
    rows = [block.shape[0] for block in blocks]

    def kernel(*refs):
        at = 0
        for ref, count in zip(refs, rows):
            refs[-1][pl.ds(at, count), :] = ref[...]
            at += count

    return local(kernel, (sum(rows), blocks[0].shape[1]), blocks)


def join(size, *terms):
    spans = [(at, rows) for _, at, rows in terms]

    def kernel(*refs):
        cut = min(rows for _, rows in spans)
        for low, high in ((0, cut), (cut, size)):
            if low < high:
                total = None
                for ref, (at, rows) in zip(refs, spans):
                    if rows >= high:
                        value = ref[pl.ds(at + low, high - low), :].astype(jnp.float32)
                        total = value if total is None else total + value
                refs[-1][pl.ds(low, high - low), :] = total.astype(refs[-1].dtype)

    return local(kernel, (size, terms[0][0].shape[1]), [array for array, _, _ in terms])


def body(tokens, counts, norm_gain, gate_weight, up_weight, down_weight):
    slots, width = tokens.shape
    members = lax.axis_size("tp")
    chips = members // 2
    part = slots // CHUNKS
    both = 2 * part

    swap_pairs = [(i, i ^ 1) for i in range(members)]
    ring_pairs = [(2 * z, 2 * ((z + 1) % chips)) for z in range(chips)]
    ring_pairs += [(2 * z + 1, 2 * ((z - 1) % chips) + 1) for z in range(chips)]

    def swap(value):
        return lax.ppermute(value, "tp", swap_pairs)

    def ring(value):
        return lax.ppermute(value, "tp", ring_pairs)

    f32 = jnp.float32
    bf16 = jnp.bfloat16
    token = counts

    def order(*values):
        nonlocal token
        token, *values = lax.optimization_barrier((token, *values))
        return values if len(values) > 1 else values[0]

    def concat(*values):
        return order(pack(*order(*values)))

    batch = {}
    gate_rows, up_rows, down_rows = gate_weight.T, up_weight.T, down_weight

    def gate_of(name):
        rows, weight = order(batch[name], gate_rows)
        batch[name] = rows, order(lax.dot_general(rows, weight, (((1,), (1,)), ((), ())), preferred_element_type=f32))

    def hidden_of(name):
        rows, gate, weight = order(*batch[name], up_rows)
        up_part = lax.dot_general(rows, weight, (((1,), (1,)), ((), ())), preferred_element_type=f32)
        batch[name] = order((jax.nn.silu(gate) * up_part).astype(bf16))

    def partial_of(name):
        hidden, weight = order(batch[name], down_rows)
        batch[name] = order(jnp.dot(hidden, weight, preferred_element_type=f32).astype(bf16))

    chunks = range(CHUNKS)
    normed = order(normalize(*order(tokens, norm_gain)))
    swapped = order(swap(normed))
    own, flight = [], []
    for i in chunks:
        rows = slice(i * part, (i + 1) * part)
        own.append(concat(normed[rows], swapped[rows]))
        flight.append(ring(own[i]))

    mine = {}
    other = {}

    def arrive(hop, i):
        block = order(flight[i])
        mine[hop, i] = block
        if hop < 3:
            flight[i] = ring(block)
        elif hop == 3:
            flight[i] = ring(block[:part])

    waiting = []

    def receive(hop, i):
        arrive(hop, i)
        if len(waiting) == 2:
            key = waiting.pop(0)
            other[key] = order(other[key])
        other[hop, i] = swap(mine[hop, i])
        waiting.append((hop, i))

    receive(1, 0)
    receive(1, 1)
    receive(1, 2)
    receive(2, 0)
    batch["a"] = concat(*own, *[mine[1, i] for i in chunks], other[1, 0], other[1, 1])
    gate_of("a")
    receive(2, 1)
    hidden_of("a")
    receive(2, 2)
    partial_of("a")
    receive(3, 0)
    receive(3, 1)
    batch["b"] = concat(other[1, 2], *[other[2, i] for i in chunks], *[mine[2, i] for i in chunks], mine[3, 0])
    gate_of("b")
    receive(3, 2)
    hidden_of("b")
    receive(4, 0)
    partial_of("b")
    receive(4, 1)
    moved_2 = swap(batch["b"][4 * both:])
    receive(4, 2)
    for key in waiting:
        other[key] = order(other[key])
    last = [other[3, i] for i in chunks] + [mine[3, 1], mine[3, 2]]
    last += [mine[4, i] for i in chunks] + [other[4, i] for i in chunks]
    batch["c"] = concat(*last)
    gate_of("c")
    hidden_of("c")
    partial_of("c")
    moved_4 = swap(batch["c"][5 * both:5 * both + 3 * part])
    moved_3 = swap(batch["c"][3 * both:5 * both])
    moved_4 = order(moved_4)
    moved_1 = None

    def depart(hop, i):
        size = part if hop == 4 else both
        terms = []
        if hop == 4:
            terms = [(batch["c"], 5 * both + 3 * part + i * part, part), (moved_4, i * part, part)]
        elif hop == 3:
            there = (moved_2, 3 * both, both) if i == 0 else (moved_3, (i - 1) * both, both)
            terms = [(batch["c"], i * both, both), there, (flight[i], 0, part)]
        elif hop == 2:
            terms = [(batch["b"], (1 + i) * both, both), (moved_2, i * both, both), (flight[i], 0, both)]
        elif hop == 1:
            here = (batch["b"], 0, both) if i == 2 else (batch["a"], (6 + i) * both, both)
            terms = [here, (moved_1, i * both, both), (flight[i], 0, both)]
        arrays = order(*[array for array, _, _ in terms])
        terms = [(array, at, rows) for array, (_, at, rows) in zip(arrays, terms)]
        flight[i] = ring(order(join(size, *terms)))

    for i in chunks:
        depart(4, i)
    moved_3 = order(moved_3)
    moved_1 = swap(batch["a"][3 * both:6 * both])
    for hop in (3, 2, 1):
        for i in chunks:
            depart(hop, i)
    given = []
    for i in chunks:
        carry, mixed = order(flight[i], batch["a"])
        flight[i] = carry
        given.append(swap(order(join(part, (mixed, i * both + part, part), (carry, 0, part)))))
    done = []
    for i in chunks:
        carry, mixed, gift = order(flight[i], batch["a"], given[i])
        done.append(carry[part:].astype(f32) + mixed[i * both:i * both + part].astype(f32) + gift.astype(f32))
    alive = jnp.arange(slots, dtype=jnp.int32) < token[0]
    return jnp.where(alive[:, None], jnp.concatenate(done, 0), 0.0).astype(bf16)


def solution(mesh):
    in_specs = (
        P(("grp", "tp"), None),
        P(("grp", "tp")),
        P(),
        P(None, "tp"),
        P(None, "tp"),
        P("tp", None),
    )
    out_specs = P(("grp", "tp"), None)
    return jax.shard_map(body, mesh=mesh, in_specs=in_specs, out_specs=out_specs, check_vma=False)
```

```python
import jax
import jax.numpy as jnp
from jax import lax
from jax.experimental import pallas as pl
from jax.experimental.pallas import tpu as pltpu
from jax.sharding import PartitionSpec as P

CHUNKS = 3
HOP_BYTES = 9_000_000
IN_VMEM = pl.BlockSpec(memory_space=pltpu.VMEM)


def local(kernel, shape, operands, specs=None, bytes_accessed=HOP_BYTES):
    return pl.pallas_call(
        kernel,
        out_shape=jax.ShapeDtypeStruct(shape, jnp.bfloat16),
        in_specs=specs or [IN_VMEM] * len(operands),
        out_specs=IN_VMEM,
        compiler_params=pltpu.CompilerParams(vmem_limit_bytes=3 << 20),
        cost_estimate=pl.CostEstimate(flops=0, bytes_accessed=bytes_accessed, transcendentals=0),
    )(*operands)


def by_columns(width, step, work):
    def one(index, none):
        work(pl.ds(pl.multiple_of(index * step, step), step))
        return none

    lax.fori_loop(0, width // step, one, 0)


def normalize(tokens, gain):
    slots, width = tokens.shape

    def kernel(tokens_ref, gain_ref, normed_ref):
        def one(index, none):
            rows = pl.ds(pl.multiple_of(index * 16, 16), 16)
            widened = tokens_ref[rows, :].astype(jnp.float32)
            scale_row = lax.rsqrt(jnp.sum(widened * widened, axis=-1, keepdims=True) / width + 1e-06)
            normed_ref[rows, :] = (widened * scale_row * gain_ref[...].reshape(1, width)).astype(normed_ref.dtype)
            return none

        lax.fori_loop(0, slots // 16, one, 0)

    return local(kernel, tokens.shape, (tokens, gain))


def pack(*blocks):
    rows = [block.shape[0] for block in blocks]

    def kernel(*refs):
        def work(columns):
            at = 0
            for ref, count in zip(refs, rows):
                refs[-1][pl.ds(at, count), columns] = ref[:, columns]
                at += count

        by_columns(blocks[0].shape[1], 512, work)

    return local(kernel, (sum(rows), blocks[0].shape[1]), blocks)


def join(size, *terms):
    spans = [(at, rows) for _, at, rows in terms]

    def kernel(*refs):
        cut = min(rows for _, rows in spans)

        def work(columns):
            for low, high in ((0, cut), (cut, size)):
                if low < high:
                    total = None
                    for ref, (at, rows) in zip(refs, spans):
                        if rows >= high:
                            value = ref[pl.ds(at + low, high - low), columns].astype(jnp.float32)
                            total = value if total is None else total + value
                    refs[-1][pl.ds(low, high - low), columns] = total.astype(refs[-1].dtype)

        by_columns(terms[0][0].shape[1], 512, work)

    return local(kernel, (size, terms[0][0].shape[1]), [array for array, _, _ in terms])


def body(tokens, counts, norm_gain, gate_weight, up_weight, down_weight):
    slots, width = tokens.shape
    members = lax.axis_size("tp")
    chips = members // 2
    part = slots // CHUNKS
    both = 2 * part

    swap_pairs = [(i, i ^ 1) for i in range(members)]
    ring_pairs = [(2 * z, 2 * ((z + 1) % chips)) for z in range(chips)]
    ring_pairs += [(2 * z + 1, 2 * ((z - 1) % chips) + 1) for z in range(chips)]

    def swap(value):
        return lax.ppermute(value, "tp", swap_pairs)

    def ring(value):
        return lax.ppermute(value, "tp", ring_pairs)

    f32 = jnp.float32
    bf16 = jnp.bfloat16
    token = counts

    def order(*values):
        nonlocal token
        token, *values = lax.optimization_barrier((token, *values))
        return values if len(values) > 1 else values[0]

    def concat(*values):
        return order(pack(*order(*values)))

    batch = {}
    gate_rows, up_rows, down_rows = gate_weight.T, up_weight.T, down_weight

    def gate_of(name):
        rows, weight = order(batch[name], gate_rows)
        batch[name] = rows, order(lax.dot_general(rows, weight, (((1,), (1,)), ((), ())), preferred_element_type=f32))

    def hidden_of(name):
        rows, gate, weight = order(*batch[name], up_rows)
        up_part = lax.dot_general(rows, weight, (((1,), (1,)), ((), ())), preferred_element_type=f32)
        batch[name] = order((jax.nn.silu(gate) * up_part).astype(bf16))

    def partial_of(name):
        hidden, weight = order(batch[name], down_rows)
        batch[name] = order(jnp.dot(hidden, weight, preferred_element_type=f32).astype(bf16))

    chunks = range(CHUNKS)
    normed = order(normalize(*order(tokens, norm_gain)))
    swapped = order(swap(normed))
    own, flight = [], []
    for i in chunks:
        rows = slice(i * part, (i + 1) * part)
        own.append(concat(normed[rows], swapped[rows]))
        flight.append(ring(own[i]))

    mine = {}
    other = {}

    def arrive(hop, i):
        block = order(flight[i])
        mine[hop, i] = block
        if hop < 3:
            flight[i] = ring(block)
        elif hop == 3:
            flight[i] = ring(block[:part])

    waiting = []

    def receive(hop, i):
        arrive(hop, i)
        if len(waiting) == 2:
            key = waiting.pop(0)
            other[key] = order(other[key])
        other[hop, i] = swap(mine[hop, i])
        waiting.append((hop, i))

    receive(1, 0)
    receive(1, 1)
    receive(1, 2)
    receive(2, 0)
    batch["a"] = concat(*own, *[mine[1, i] for i in chunks], other[1, 0], other[1, 1])
    gate_of("a")
    receive(2, 1)
    hidden_of("a")
    receive(2, 2)
    partial_of("a")
    receive(3, 0)
    receive(3, 1)
    batch["b"] = concat(other[1, 2], *[other[2, i] for i in chunks], *[mine[2, i] for i in chunks], mine[3, 0])
    gate_of("b")
    receive(3, 2)
    hidden_of("b")
    arrive(4, 0)
    key = waiting.pop(0)
    other[key] = order(other[key])
    partial_of("b")
    arrive(4, 1)
    moved_2 = swap(batch["b"][4 * both:])
    arrive(4, 2)
    key = waiting.pop(0)
    other[key] = order(other[key])
    fourth = concat(*[mine[4, i] for i in chunks])
    fifth = order(swap(fourth))
    last = [other[3, i] for i in chunks] + [mine[3, 1], mine[3, 2]]
    batch["c"] = concat(*last, fourth, fifth)
    gate_of("c")
    hidden_of("c")
    partial_of("c")
    moved_4 = order(swap(batch["c"][3 * both:5 * both + 3 * part]))
    moved_1 = None

    def depart(hop, i):
        size = part if hop == 4 else both
        terms = []
        if hop == 4:
            terms = [(batch["c"], 5 * both + 3 * part + i * part, part), (moved_4, 2 * both + i * part, part)]
        elif hop == 3:
            there = (moved_2, 3 * both, both) if i == 0 else (moved_4, (i - 1) * both, both)
            terms = [(batch["c"], i * both, both), there, (flight[i], 0, part)]
        elif hop == 2:
            terms = [(batch["b"], (1 + i) * both, both), (moved_2, i * both, both), (flight[i], 0, both)]
        elif hop == 1:
            here = (batch["b"], 0, both) if i == 2 else (batch["a"], (6 + i) * both, both)
            terms = [here, (moved_1, i * both, both), (flight[i], 0, both)]
        arrays = order(*[array for array, _, _ in terms])
        terms = [(array, at, rows) for array, (_, at, rows) in zip(arrays, terms)]
        flight[i] = ring(order(join(size, *terms)))

    for i in chunks:
        depart(4, i)
    moved_1 = swap(batch["a"][3 * both:6 * both])
    for hop in (3, 2, 1):
        for i in chunks:
            depart(hop, i)
    given = []
    for i in chunks:
        carry, mixed = order(flight[i], batch["a"])
        flight[i] = carry
        given.append(swap(order(join(part, (mixed, i * both + part, part), (carry, 0, part)))))
    done = []
    for i in chunks:
        carry, mixed, gift = order(flight[i], batch["a"], given[i])
        done.append(carry[part:].astype(f32) + mixed[i * both:i * both + part].astype(f32) + gift.astype(f32))
    alive = jnp.arange(slots, dtype=jnp.int32) < token[0]
    return jnp.where(alive[:, None], jnp.concatenate(done, 0), 0.0).astype(bf16)


def solution(mesh):
    in_specs = (
        P(("grp", "tp"), None),
        P(("grp", "tp")),
        P(),
        P(None, "tp"),
        P(None, "tp"),
        P("tp", None),
    )
    out_specs = P(("grp", "tp"), None)
    return jax.shard_map(body, mesh=mesh, in_specs=in_specs, out_specs=out_specs, check_vma=False)
```

```python
import jax
import jax.numpy as jnp
from jax import lax
from jax.experimental import pallas as pl
from jax.experimental.pallas import tpu as pltpu
from jax.sharding import PartitionSpec as P

CHUNKS = 3
HOP_BYTES = 9_000_000
IN_VMEM = pl.BlockSpec(memory_space=pltpu.VMEM)


def local(kernel, shape, operands, specs=None, bytes_accessed=HOP_BYTES):
    return pl.pallas_call(
        kernel,
        out_shape=jax.ShapeDtypeStruct(shape, jnp.bfloat16),
        in_specs=specs or [IN_VMEM] * len(operands),
        out_specs=IN_VMEM,
        compiler_params=pltpu.CompilerParams(vmem_limit_bytes=3 << 20),
        cost_estimate=pl.CostEstimate(flops=0, bytes_accessed=bytes_accessed, transcendentals=0),
    )(*operands)


def by_columns(width, step, work):
    def one(index, none):
        work(pl.ds(pl.multiple_of(index * step, step), step))
        return none

    lax.fori_loop(0, width // step, one, 0)


def normalize(tokens, gain):
    slots, width = tokens.shape

    def kernel(tokens_ref, gain_ref, normed_ref):
        def one(index, none):
            rows = pl.ds(pl.multiple_of(index * 16, 16), 16)
            widened = tokens_ref[rows, :].astype(jnp.float32)
            scale_row = lax.rsqrt(jnp.sum(widened * widened, axis=-1, keepdims=True) / width + 1e-06)
            normed_ref[rows, :] = (widened * scale_row * gain_ref[...].reshape(1, width)).astype(normed_ref.dtype)
            return none

        lax.fori_loop(0, slots // 16, one, 0)

    return local(kernel, tokens.shape, (tokens, gain))


def pack(*blocks):
    rows = [block.shape[0] for block in blocks]

    def kernel(*refs):
        def work(columns):
            at = 0
            for ref, count in zip(refs, rows):
                refs[-1][pl.ds(at, count), columns] = ref[:, columns]
                at += count

        by_columns(blocks[0].shape[1], 512, work)

    return local(kernel, (sum(rows), blocks[0].shape[1]), blocks)


def join(size, *terms):
    spans = [(at, rows) for _, at, rows in terms]

    def kernel(*refs):
        cut = min(rows for _, rows in spans)

        def work(columns):
            for low, high in ((0, cut), (cut, size)):
                if low < high:
                    total = None
                    for ref, (at, rows) in zip(refs, spans):
                        if rows >= high:
                            value = ref[pl.ds(at + low, high - low), columns].astype(jnp.float32)
                            total = value if total is None else total + value
                    refs[-1][pl.ds(low, high - low), columns] = total.astype(refs[-1].dtype)

        by_columns(terms[0][0].shape[1], 512, work)

    return local(kernel, (size, terms[0][0].shape[1]), [array for array, _, _ in terms])


def body(tokens, counts, norm_gain, gate_weight, up_weight, down_weight):
    slots, width = tokens.shape
    members = lax.axis_size("tp")
    chips = members // 2
    part = slots // CHUNKS
    both = 2 * part

    swap_pairs = [(i, i ^ 1) for i in range(members)]
    ring_pairs = [(2 * z, 2 * ((z + 1) % chips)) for z in range(chips)]
    ring_pairs += [(2 * z + 1, 2 * ((z - 1) % chips) + 1) for z in range(chips)]

    def swap(value):
        return lax.ppermute(value, "tp", swap_pairs)

    def ring(value):
        return lax.ppermute(value, "tp", ring_pairs)

    f32 = jnp.float32
    bf16 = jnp.bfloat16
    token = counts

    def order(*values):
        nonlocal token
        token, *values = lax.optimization_barrier((token, *values))
        return values if len(values) > 1 else values[0]

    def concat(*values):
        return order(pack(*order(*values)))

    batch = {}
    gate_rows, up_rows, down_rows = gate_weight.T, up_weight.T, down_weight

    def gate_of(name):
        rows, weight = order(batch[name], gate_rows)
        batch[name] = rows, order(lax.dot_general(rows, weight, (((1,), (1,)), ((), ())), preferred_element_type=f32))

    def hidden_of(name):
        rows, gate, weight = order(*batch[name], up_rows)
        up_part = lax.dot_general(rows, weight, (((1,), (1,)), ((), ())), preferred_element_type=f32)
        batch[name] = order((jax.nn.silu(gate) * up_part).astype(bf16))

    def partial_of(name):
        hidden, weight = order(batch[name], down_rows)
        batch[name] = order(jnp.dot(hidden, weight, preferred_element_type=f32).astype(bf16))

    chunks = range(CHUNKS)
    raw = swap(tokens)
    normed = order(normalize(*order(tokens, norm_gain)))
    swapped = order(normalize(*order(raw, norm_gain)))
    own, flight = [], []
    for i in chunks:
        rows = slice(i * part, (i + 1) * part)
        own.append(concat(normed[rows], swapped[rows]))
        flight.append(ring(own[i]))

    mine = {}
    other = {}

    def arrive(hop, i):
        block = order(flight[i])
        mine[hop, i] = block
        if hop < 3:
            flight[i] = ring(block)
        elif hop == 3:
            flight[i] = ring(block[:part])

    waiting = []

    def receive(hop, i):
        arrive(hop, i)
        if len(waiting) == 2:
            key = waiting.pop(0)
            other[key] = order(other[key])
        other[hop, i] = swap(mine[hop, i])
        waiting.append((hop, i))

    receive(1, 0)
    receive(1, 1)
    receive(1, 2)
    receive(2, 0)
    batch["a"] = concat(*own, *[mine[1, i] for i in chunks], other[1, 0], other[1, 1])
    gate_of("a")
    receive(2, 1)
    hidden_of("a")
    receive(2, 2)
    partial_of("a")
    receive(3, 0)
    receive(3, 1)
    batch["b"] = concat(other[1, 2], *[other[2, i] for i in chunks], *[mine[2, i] for i in chunks], mine[3, 0])
    gate_of("b")
    receive(3, 2)
    hidden_of("b")
    arrive(4, 0)
    key = waiting.pop(0)
    other[key] = order(other[key])
    partial_of("b")
    arrive(4, 1)
    moved_2 = swap(batch["b"][4 * both:])
    arrive(4, 2)
    key = waiting.pop(0)
    other[key] = order(other[key])
    fourth = concat(*[mine[4, i] for i in chunks])
    fifth = order(swap(fourth))
    last = [other[3, i] for i in chunks] + [mine[3, 1], mine[3, 2]]
    batch["c"] = concat(*last, fourth, fifth)
    gate_of("c")
    hidden_of("c")
    partial_of("c")
    moved_4 = order(swap(batch["c"][3 * both:5 * both + 3 * part]))
    moved_1 = None

    def depart(hop, i):
        size = part if hop == 4 else both
        terms = []
        if hop == 4:
            terms = [(batch["c"], 5 * both + 3 * part + i * part, part), (moved_4, 2 * both + i * part, part)]
        elif hop == 3:
            there = (moved_2, 3 * both, both) if i == 0 else (moved_4, (i - 1) * both, both)
            terms = [(batch["c"], i * both, both), there, (flight[i], 0, part)]
        elif hop == 2:
            terms = [(batch["b"], (1 + i) * both, both), (moved_2, i * both, both), (flight[i], 0, both)]
        elif hop == 1:
            here = (batch["b"], 0, both) if i == 2 else (batch["a"], (6 + i) * both, both)
            terms = [here, (moved_1, i * both, both), (flight[i], 0, both)]
        arrays = order(*[array for array, _, _ in terms])
        terms = [(array, at, rows) for array, (_, at, rows) in zip(arrays, terms)]
        flight[i] = ring(order(join(size, *terms)))

    for i in chunks:
        depart(4, i)
    moved_1 = swap(batch["a"][3 * both:6 * both])
    for hop in (3, 2, 1):
        for i in chunks:
            depart(hop, i)
    given = []
    for i in chunks:
        carry, mixed = order(flight[i], batch["a"])
        flight[i] = carry
        given.append(swap(order(join(part, (mixed, i * both + part, part), (carry, 0, part)))))
    done = []
    for i in chunks:
        carry, mixed, gift = order(flight[i], batch["a"], given[i])
        done.append(carry[part:].astype(f32) + mixed[i * both:i * both + part].astype(f32) + gift.astype(f32))
    alive = jnp.arange(slots, dtype=jnp.int32) < token[0]
    return jnp.where(alive[:, None], jnp.concatenate(done, 0), 0.0).astype(bf16)


def solution(mesh):
    in_specs = (
        P(("grp", "tp"), None),
        P(("grp", "tp")),
        P(),
        P(None, "tp"),
        P(None, "tp"),
        P("tp", None),
    )
    out_specs = P(("grp", "tp"), None)
    return jax.shard_map(body, mesh=mesh, in_specs=in_specs, out_specs=out_specs, check_vma=False)
```
